32 devices in a mesh: dp: 4 (over y, x), expert: 8 (over z, core).
Axes of the slice: x: 2, y: 2, z: 4, core: 2. Of those that a mesh axis runs over, the one named last changes fastest.
Arguments:
- tokens: bfloat16 [4096, 2048], P(('dp', 'expert')), may hold values from -6 to 6
- cotangent: bfloat16 [4096, 2048], P(('dp', 'expert')), may hold values from -6 to 6
- expert_ids: int32 [4096, 4], P(('dp', 'expert')), may hold values from 0 to 7, all different within a row; in each aligned block of 128 rows (0 to 127, 128 to 255, ...) at most 80 rows name the same one
- gate_probs: bfloat16 [4096, 4], P(('dp', 'expert')), may hold values from 0.049804688 to 1
- w_gate: bfloat16 [8, 2048, 512], P('expert', 'dp'), may hold values from -0.125 to 0.125
- w_up: bfloat16 [8, 2048, 512], P('expert', 'dp'), may hold values from -0.125 to 0.125
- w_down: bfloat16 [8, 512, 2048], P('expert', None, 'dp'), may hold values from -0.25 to 0.25
Outputs:
- mixed: bfloat16 [4096, 2048], P(('dp', 'expert'))
- grad_tokens: bfloat16 [4096, 2048], P(('dp', 'expert'))
- grad_gates: float32 [4096, 4], P(('dp', 'expert'))
- grad_gate_w: float32 [8, 2048, 512], P('expert', 'dp')
- grad_up_w: float32 [8, 2048, 512], P('expert', 'dp')
- grad_down_w: float32 [8, 512, 2048], P('expert', None, 'dp')
The draws below stay inside these ranges and needn't reach their ends.
Inputs may be any that keep to these rules, and one draw needn't show every extreme that they name: `expert_ids`: each row names 4 different experts. Within the rows of one device (aligned blocks of 128 rows) no expert is named by more than 80 rows, a bound that some block reaches.
All inputs are finite; a program needn't handle non-finite values.
Results may differ from the reference program's by a relative error of at most 0.0085.
Values may be sent and summed in bfloat16 or wider, within the bound.
A program may use at most 128 MiB of HBM per device.

```python
import math
import jax
import jax.numpy as jnp
import numpy as np
from jax import lax

D = 2048
FW = 512
TOPK = 4
TOK_DEV = 128
EXPERTS = 8
TOKENS = 4096
CAP = 80
N_DP = 4
N_EXPERT = 8


def steps_of(key, shape, pieces, smallest, top_value):
    gain, own = 1.0, jax.random.fold_in(key, 6)
    for dim, shards_of in pieces:
        draws = jnp.exp(jax.random.uniform(jax.random.fold_in(own, dim), (shards_of,), jnp.float32, smallest / len(pieces), top_value / len(pieces)))
        gain = gain * jnp.repeat(draws, shape[dim] // shards_of).reshape([-1 if axis == dim else 1 for axis in range(len(shape))])
    return gain


def routed_block(stream_key, own, number, rows, amount, top, bound, skew):
    sequence = jax.random.permutation(stream_key, amount)
    heavy_load, ordinary = portions_of(amount, rows * top, bound, skew, True), portions_of(amount, rows * top, bound, skew, False)
    places = jnp.arange(amount)

    def named(sizes, offset_by):
        used = int((sizes > 0).sum())
        fixed = max(1, used // 4)
        passed = fixed + (places - fixed + offset_by * (used - fixed)) % max(1, amount - fixed)
        return jnp.zeros((amount,), jnp.int32).at[sequence[jnp.where(places < fixed, places, passed)]].set(jnp.asarray(sizes, jnp.int32))

    sizes = jnp.where(number % 4 == 0, named(heavy_load, number // 4), named(ordinary, number - number // 4 - 1))
    mixed = jax.random.permutation(jax.random.fold_in(own, 3), amount)
    donor, sink = mixed[0:amount // 2 * 2:2], mixed[1:amount // 2 * 2:2]
    slack = jnp.minimum(sizes[donor] - 1, bound - sizes[sink]) // 2
    slack = jnp.where((donor == sequence[0]) | (sink == sequence[0]) | (sizes[sink] == 0), 0, jnp.maximum(slack, 0))
    passed = jax.random.randint(jax.random.fold_in(own, 4), (amount // 2,), 0, 1 << 20) % (slack + 1)
    sizes = sizes.at[donor].add(-passed).at[sink].add(passed)
    members = jnp.searchsorted(jnp.cumsum(sizes), jnp.arange(rows * top), side="right").astype(jnp.int32)
    listing = members.reshape(top, rows).T
    listing = listing[jax.random.permutation(jax.random.fold_in(own, 1), rows)]
    offset_by = jax.random.randint(jax.random.fold_in(own, 2), (rows, 1), 0, top)
    return jnp.take_along_axis(listing, (jnp.arange(top)[None, :] + offset_by) % top, axis=1)


def portions_of(count, total, reach, lean, full):
    weights = [(1 << 20) // math.isqrt(standing ** lean) + 1 for standing in range(1, count + 1)]
    largest = reach if full else min(reach, max(-(-total // count), total * weights[0] // sum(weights)))
    least = 1 if total - largest >= count - 1 else 0
    counts, surplus = [largest] + [least] * (count - 1), total - largest - least * (count - 1)
    while surplus > 0:
        movable = [i for i in range(1, count) if counts[i] < largest] or [i for i in range(1, count) if counts[i] < reach]
        mass, remaining = sum([weights[i] for i in movable]), surplus
        for i in movable:
            extra = min(reach - counts[i], max(1, remaining * weights[i] // mass), surplus)
            counts[i] = counts[i] + extra
            surplus = surplus - extra
    return np.array(counts)


def noise(rng, dims, deviation, bound, pieces=(), kind=jnp.bfloat16):
    loudness = steps_of(rng, dims, pieces, -0.22, 0.18) if pieces else 1.0
    drawn = jax.random.normal(rng, dims, jnp.float32) * deviation * loudness
    return jnp.minimum(jnp.maximum(drawn, -bound), bound).astype(kind)


def setup_inputs(seed: int = 0) -> dict:
    key_list = jax.random.split(jax.random.key(seed), 8)
    tokens = noise(key_list[0], (TOKENS, D), 1.0, 6.0, ((0, 32),))
    cotangent = noise(key_list[1], (TOKENS, D), 1.0, 6.0, ((0, 32),))
    expert_ids_keys = jax.random.split(jax.random.fold_in(key_list[2], 1), TOKENS // TOK_DEV)
    expert_ids_turns = jax.random.permutation(jax.random.fold_in(key_list[2], 3), TOKENS // TOK_DEV)
    expert_ids = jax.vmap(lambda own, number: routed_block(jax.random.fold_in(key_list[2], 2), own, number, TOK_DEV, EXPERTS, TOPK, CAP, 2))(expert_ids_keys, expert_ids_turns).reshape((TOKENS, TOPK))
    gate_probs = jnp.clip(jnp.exp(math.log(1.0) - 2.9996462 * jax.random.uniform(key_list[3], (TOKENS, TOPK), jnp.float32) ** steps_of(key_list[3], (TOKENS, TOPK), ((0, 32),), -0.2, 0.2)), 0.049804688, 1.0).astype(jnp.bfloat16)
    w_gate = noise(key_list[4], (EXPERTS, D, FW), D ** -0.5, 0.125, ((0, 8), (1, 4)))
    w_up = noise(key_list[5], (EXPERTS, D, FW), D ** -0.5, 0.125, ((0, 8), (1, 4)))
    w_down = noise(key_list[6], (EXPERTS, FW, D), FW ** -0.5, 0.25, ((0, 8), (2, 4)))
    return {"tokens": tokens, "cotangent": cotangent, "expert_ids": expert_ids, "gate_probs": gate_probs, "w_gate": w_gate, "w_up": w_up, "w_down": w_down}


def silu_parts(pre_gate):
    sigma = jax.nn.sigmoid(pre_gate)
    return pre_gate * sigma, sigma * (1.0 + pre_gate * (1.0 - sigma))


def settle(partials):
    rounded = lax.optimization_barrier(partials.astype(jnp.bfloat16))
    return jnp.sum(rounded.astype(jnp.float32), axis=0)


def place_block(table_row, positions, values):
    return table_row.at[positions].set(values)


def reference(tokens, cotangent, expert_ids, gate_probs, w_gate, w_up, w_down):
    blocks = N_DP * N_EXPERT
    per_block = TOK_DEV * TOPK
    ids = expert_ids.reshape(blocks, per_block).astype(jnp.int32)
    onehot = (ids[:, :, None] == jnp.arange(EXPERTS, dtype=jnp.int32)[None, None, :]).astype(jnp.int32)
    earlier = jnp.cumsum(onehot, axis=1) - onehot
    slot_rank = jnp.sum(earlier * onehot, axis=2).astype(jnp.int32)
    position = (ids * CAP + slot_rank).astype(jnp.int32)
    pair_index = jnp.arange(blocks * per_block, dtype=jnp.int32).reshape(blocks, per_block)
    sentinel = TOKENS * TOPK
    table = jnp.full((blocks, EXPERTS * CAP), sentinel, jnp.int32)
    table = jax.vmap(place_block)(table, position, pair_index)
    table = table.reshape(blocks, EXPERTS, CAP).transpose(1, 0, 2).reshape(EXPERTS, N_DP, N_EXPERT * CAP)
    gate_flat = gate_probs.reshape(-1).astype(jnp.float32)

    def expert_pass(carry, inputs):
        mixed_acc, grad_acc, gates_acc = carry
        pairs, gate_w, up_w, down_w = inputs
        tok_index = (pairs // TOPK).astype(jnp.int32)
        rows_in = jnp.take(tokens, tok_index, axis=0, mode="fill", fill_value=0).astype(jnp.float32)
        cot_rows = jnp.take(cotangent, tok_index, axis=0, mode="fill", fill_value=0).astype(jnp.float32)
        weights = jnp.take(gate_flat, pairs, axis=0, mode="fill", fill_value=0)
        routed = (weights[:, :, None] * cot_rows).astype(jnp.bfloat16).astype(jnp.float32)
        gate_f = gate_w.astype(jnp.float32)
        up_f = up_w.astype(jnp.float32)
        down_f = down_w.astype(jnp.float32)
        pre_gate = jnp.einsum("qnd,df->qnf", rows_in, gate_f)
        pre_up = jnp.einsum("qnd,df->qnf", rows_in, up_f)
        activated, slope = silu_parts(pre_gate)
        hidden = (activated * pre_up).astype(jnp.bfloat16).astype(jnp.float32)
        expert_out = jnp.einsum("qnf,fd->qnd", hidden, down_f).astype(jnp.bfloat16).astype(jnp.float32)
        grad_hidden = jnp.einsum("qnd,fd->qnf", routed, down_f)
        grad_pre_gate = (grad_hidden * pre_up * slope).astype(jnp.bfloat16).astype(jnp.float32)
        grad_pre_up = (grad_hidden * activated).astype(jnp.bfloat16).astype(jnp.float32)
        pair_grad = (jnp.einsum("qnf,df->qnd", grad_pre_gate, gate_f) + jnp.einsum("qnf,df->qnd", grad_pre_up, up_f)).astype(jnp.bfloat16).astype(jnp.float32)
        mixed_acc = mixed_acc.at[tok_index].add(weights[:, :, None] * expert_out, mode="drop")
        grad_acc = grad_acc.at[tok_index].add(pair_grad, mode="drop")
        gates_acc = gates_acc.at[pairs].add(jnp.sum(cot_rows * expert_out, axis=-1), mode="drop")
        grad_gate_e = settle(jnp.einsum("qnd,qnf->qdf", rows_in, grad_pre_gate))
        grad_up_e = settle(jnp.einsum("qnd,qnf->qdf", rows_in, grad_pre_up))
        grad_down_e = settle(jnp.einsum("qnf,qnd->qfd", hidden, routed))
        return (mixed_acc, grad_acc, gates_acc), (grad_gate_e, grad_up_e, grad_down_e)

    start = (jnp.zeros((TOKENS, D), jnp.float32), jnp.zeros((TOKENS, D), jnp.float32), jnp.zeros((TOKENS * TOPK,), jnp.float32))
    final, grads = lax.scan(expert_pass, start, (table, w_gate, w_up, w_down))
    mixed_acc, grad_acc, gates_acc = final
    return (mixed_acc.astype(jnp.bfloat16), grad_acc.astype(jnp.bfloat16), gates_acc.reshape(TOKENS, TOPK), grads[0], grads[1], grads[2])
```

```python
import functools

import jax
import jax.numpy as jnp
from jax import lax
from jax.experimental import pallas as pl
from jax.experimental.pallas import tpu as pltpu
from jax.sharding import PartitionSpec as P


def silu_parts(pre_gate):
    sigma = jax.nn.sigmoid(pre_gate)
    return (pre_gate * sigma, sigma * (1.0 + pre_gate * (1.0 - sigma)))


def on_device_routed(tokens, cotangent, expert_ids, gate_probs, w_gate, w_up, w_down):
    axis_count = lax.axis_size("expert")
    local_experts = w_gate.shape[0]
    tok_rows = tokens.shape[0]
    model_width = tokens.shape[1]
    top_count = expert_ids.shape[1]
    all_experts = local_experts * axis_count
    capacity = max(2, 5 * tok_rows * top_count // (4 * all_experts))
    pair_count = tok_rows * top_count
    flat_ids = expert_ids.reshape(-1)
    onehot = (flat_ids[:, None] == jnp.arange(all_experts, dtype=jnp.int32)[None, :]).astype(
        jnp.int32
    )
    before = jnp.tril(jnp.ones((pair_count, pair_count), jnp.bfloat16), -1)
    earlier = jnp.dot(
        before, onehot.astype(jnp.bfloat16), preferred_element_type=jnp.float32
    ).astype(jnp.int32)
    slot_rank = jnp.sum(earlier * onehot, axis=1)
    position = flat_ids * capacity + slot_rank
    pair_table = jnp.full((all_experts * capacity,), pair_count, jnp.int32)
    pair_table = pair_table.at[position].set(jnp.arange(pair_count, dtype=jnp.int32))
    routed = (
        gate_probs.astype(jnp.float32)[:, :, None] * cotangent.astype(jnp.float32)[:, None, :]
    ).astype(jnp.bfloat16)
    routed = routed.reshape(pair_count, model_width)
    send_shape = (axis_count, local_experts, capacity, model_width)
    token_send = jnp.take(
        tokens, pair_table // top_count, axis=0, mode="fill", fill_value=0
    ).reshape(send_shape)
    routed_send = jnp.take(routed, pair_table, axis=0, mode="fill", fill_value=0).reshape(
        send_shape
    )
    token_recv, routed_recv = (
        lax.all_to_all(token_send, "expert", split_axis=0, concat_axis=2, tiled=True),
        lax.all_to_all(routed_send, "expert", split_axis=0, concat_axis=2, tiled=True),
    )
    rows_in = token_recv[0]
    routed_in = routed_recv[0]
    full_gate, full_up, full_down = (
        lax.all_gather(w_gate, "dp", axis=1, tiled=True),
        lax.all_gather(w_up, "dp", axis=1, tiled=True),
        lax.all_gather(w_down, "dp", axis=2, tiled=True),
    )
    pre_gate = jnp.einsum("end,edf->enf", rows_in, full_gate, preferred_element_type=jnp.float32)
    pre_up = jnp.einsum("end,edf->enf", rows_in, full_up, preferred_element_type=jnp.float32)
    activated, slope = silu_parts(pre_gate)
    hidden = (activated * pre_up).astype(jnp.bfloat16)
    expert_out = jnp.einsum(
        "enf,efd->end", hidden, full_down, preferred_element_type=jnp.float32
    ).astype(jnp.bfloat16)
    grad_hidden = jnp.einsum(
        "end,efd->enf", routed_in, full_down, preferred_element_type=jnp.float32
    )
    grad_pre_gate = (grad_hidden * pre_up * slope).astype(jnp.bfloat16)
    grad_pre_up = (grad_hidden * activated).astype(jnp.bfloat16)
    pair_grad = jnp.einsum(
        "enf,edf->end", grad_pre_gate, full_gate, preferred_element_type=jnp.float32
    )
    pair_grad = pair_grad + jnp.einsum(
        "enf,edf->end", grad_pre_up, full_up, preferred_element_type=jnp.float32
    )
    pair_grad = pair_grad.astype(jnp.bfloat16)
    back_out, back_grad = (
        lax.all_to_all(expert_out[None], "expert", split_axis=2, concat_axis=0, tiled=True),
        lax.all_to_all(pair_grad[None], "expert", split_axis=2, concat_axis=0, tiled=True),
    )
    out_pairs = back_out.reshape(all_experts * capacity, model_width)[position].reshape(
        tok_rows, top_count, model_width
    )
    grad_pairs = back_grad.reshape(all_experts * capacity, model_width)[position].reshape(
        tok_rows, top_count, model_width
    )
    mixed = jnp.einsum(
        "tk,tkd->td", gate_probs, out_pairs, preferred_element_type=jnp.float32
    ).astype(jnp.bfloat16)
    grad_gates = jnp.einsum("td,tkd->tk", cotangent, out_pairs, preferred_element_type=jnp.float32)
    grad_tokens = jnp.sum(grad_pairs.astype(jnp.float32), axis=1).astype(jnp.bfloat16)
    part_gate = jnp.einsum(
        "end,enf->edf", rows_in, grad_pre_gate, preferred_element_type=jnp.float32
    )
    part_up = jnp.einsum("end,enf->edf", rows_in, grad_pre_up, preferred_element_type=jnp.float32)
    part_down = jnp.einsum("enf,end->efd", hidden, routed_in, preferred_element_type=jnp.float32)
    grad_gate_w, grad_up_w, grad_down_w = (
        lax.psum_scatter(
            part_gate.astype(jnp.bfloat16), "dp", scatter_dimension=1, tiled=True
        ).astype(jnp.float32),
        lax.psum_scatter(
            part_up.astype(jnp.bfloat16), "dp", scatter_dimension=1, tiled=True
        ).astype(jnp.float32),
        lax.psum_scatter(
            part_down.astype(jnp.bfloat16), "dp", scatter_dimension=2, tiled=True
        ).astype(jnp.float32),
    )
    return (mixed, grad_tokens, grad_gates, grad_gate_w, grad_up_w, grad_down_w)


MESH = pl.DeviceIdType.MESH
CHIPS = 4


def places():
    q, e = lax.axis_index("dp"), lax.axis_index("expert")
    z, c = e // 2, e % 2
    x, y = q % 2, q // 2
    xn, yn, dn = 2 * y + 1 - x, 2 * (1 - y) + x, 2 * (1 - y) + 1 - x
    return q, e, z, c, xn, yn, dn


def greet(q, e, z, c, dp_peers):
    barrier = pltpu.get_barrier_semaphore()

    def hello(dev):
        pl.semaphore_signal(barrier, inc=1, device_id=dev, device_id_type=MESH)

    pl.when(z > 0)(lambda: hello((q, e - 2)))
    pl.when(z < CHIPS - 1)(lambda: hello((q, e + 2)))
    hello((q, 2 * z + 1 - c))
    for p in dp_peers:
        hello((p, e))
    line = jnp.where(z > 0, 1, 0) + jnp.where(z < CHIPS - 1, 1, 0)
    pl.semaphore_wait(barrier, line + (1 + len(dp_peers)))


def remote(src, dst, send, recv, dev):
    return pltpu.make_async_remote_copy(
        src_ref=src, dst_ref=dst, send_sem=send, recv_sem=recv, device_id=dev, device_id_type=MESH
    )


def shard_of(ref, q, start=0, rows=None):
    rows = ref.shape[-2] if rows is None else rows
    if len(ref.shape) == 3:
        return ref.at[q, pl.ds(start, rows)]
    width = ref.shape[1] // 4
    return ref.at[pl.ds(start, rows), pl.ds(pl.multiple_of(q * width, 128), width)]


def gather_kernel(*refs):
    ins, ws = refs[0:3], refs[3:6]
    alls, wall = refs[6:9], refs[9:12]
    own_sem, w_own, line_s, line_r, sib_s, sib_r, ws_s, ws_r = refs[12:]
    q, e, z, c, xn, yn, dn = places()
    sib = (q, 2 * z + 1 - c)
    greet(q, e, z, c, (xn, yn))

    half = ws[0].shape[0] // 2
    w_sends = []
    for w in range(3):
        for k, p in enumerate((xn, yn)):
            cp = remote(ws[w], shard_of(wall[w], q), ws_s.at[w, k], ws_r.at[w, k], (p, e))
            cp.start()
            w_sends.append(cp)

    def block(a, zs, core):
        return alls[a].at[2 * zs + core]

    def source(a, zs, d):
        return ins[a] if d == 0 else block(a, zs, c)

    def line_copy(a, dr, d):
        zs, to = (z - d, e + 2) if dr == 0 else (z + d, e - 2)
        return remote(
            source(a, zs, d), block(a, zs, c), line_s.at[a, dr, d], line_r.at[a, dr, d], (q, to)
        )

    def sib_copy(a, dr, d):
        zs = z - d if dr == 0 else z + d
        return remote(source(a, zs, d), block(a, zs, c), sib_s.at[a, dr, d], sib_r.at[a, dr, d], sib)

    def has_block(dr, d):
        return z - d >= 0 if dr == 0 else z + d <= CHIPS - 1

    def forwards(dr, d):
        return (
            jnp.logical_and(z - d >= 0, z < CHIPS - 1)
            if dr == 0
            else jnp.logical_and(z + d <= CHIPS - 1, z > 0)
        )

    locals_ = []
    for d in range(CHIPS):
        for a in range(3):
            for dr in range(2):
                if d > 0:

                    @pl.when(has_block(dr, d))
                    def _():
                        zs = z - d if dr == 0 else z + d
                        remote(
                            block(a, zs, c),
                            block(a, zs, c),
                            line_s.at[a, dr, d - 1],
                            line_r.at[a, dr, d - 1],
                            sib,
                        ).wait_recv()

                if d < CHIPS - 1:
                    pl.when(forwards(dr, d))(lambda: line_copy(a, dr, d).start())
                if d > 0:
                    pl.when(has_block(dr, d))(lambda: sib_copy(a, dr, d).start())
                elif dr == 0:
                    sib_copy(a, 0, 0).start()
        if d == 0:
            for a in range(3):
                cp = pltpu.make_async_copy(ins[a], alls[a].at[e], own_sem.at[a])
                cp.start()
                locals_.append(cp)
            for w in range(3):
                cp = pltpu.make_async_copy(ws[w], shard_of(wall[w], q), w_own.at[w])
                cp.start()
                locals_.append(cp)
        if d == 1:
            for w in range(3):
                for k, (p, other) in enumerate(((xn, yn), (yn, xn))):
                    whole = shard_of(wall[w], p)
                    remote(whole, whole, ws_s.at[w, k], ws_r.at[w, k], (p, e)).wait_recv()
                    part = shard_of(wall[w], p, half * k, half)
                    cp = remote(part, part, ws_s.at[w, 2 + k], ws_r.at[w, 2 + k], (other, e))
                    cp.start()
                    w_sends.append(cp)
    for cp in locals_:
        cp.wait()
    for w in range(3):
        for k in range(2):
            part = shard_of(wall[w], dn, half * k, half)
            remote(part, part, ws_s.at[w, 2 + k], ws_r.at[w, 2 + k], (xn, e)).wait_recv()
    for cp in w_sends:
        cp.wait_send()
    for d in range(CHIPS):
        for a in range(3):
            for dr in range(2):
                if d < CHIPS - 1:
                    pl.when(forwards(dr, d))(lambda: line_copy(a, dr, d).wait_send())
                if d == 0 and dr == 1:
                    continue

                @pl.when(has_block(dr, d))
                def _():
                    zs = z - d if dr == 0 else z + d
                    sib_copy(a, dr, d).wait_send()
                    got = block(a, zs, 1 - c)
                    remote(got, got, sib_s.at[a, dr, d], sib_r.at[a, dr, d], sib).wait_recv()


def gather_all(tokens, cotangent, weights_t, w_gate, w_up, w_down):
    rows, width = tokens.shape
    n = weights_t.shape[0]
    depth, hid = w_gate.shape
    any_ = pl.BlockSpec(memory_space=pl.ANY)
    dma = pltpu.SemaphoreType.DMA
    return pl.pallas_call(
        gather_kernel,
        out_shape=(
            jax.ShapeDtypeStruct((n, rows, width), tokens.dtype),
            jax.ShapeDtypeStruct((n, rows, width), tokens.dtype),
            jax.ShapeDtypeStruct((n,) + weights_t.shape, weights_t.dtype),
            jax.ShapeDtypeStruct((4, depth, hid), w_gate.dtype),
            jax.ShapeDtypeStruct((4, depth, hid), w_gate.dtype),
            jax.ShapeDtypeStruct((hid, 4 * depth), w_gate.dtype),
        ),
        in_specs=[any_] * 6,
        out_specs=(any_,) * 6,
        scratch_shapes=[
            dma((3,)),
            dma((3,)),
            dma((3, 2, 3)),
            dma((3, 2, 3)),
            dma((3, 2, 4)),
            dma((3, 2, 4)),
            dma((3, 4)),
            dma((3, 4)),
        ],
        compiler_params=pltpu.CompilerParams(collective_id=0, has_side_effects=True),
    )(tokens, cotangent, weights_t, w_gate, w_up, w_down)


def reduce_kernel(*refs):
    parts, wp = refs[0:3], refs[3:6]
    outs, wout = refs[6:9], refs[9:12]
    srecv, lrecv, wrecv = refs[12:15], refs[15:18], refs[18:21]
    sib_s, sib_r, line_s, line_r, w_s, w_r = refs[21:]
    q, e, z, c, xn, yn, dn = places()
    sib = (q, 2 * z + 1 - c)
    peers = (xn, yn, dn)
    greet(q, e, z, c, peers)

    def sib_copy(a, i):
        dest = CHIPS - 1 - i // 2 if i % 2 == 0 else i // 2
        return remote(
            parts[a].at[2 * dest + 1 - c], srecv[a].at[dest], sib_s.at[a, dest], sib_r.at[a, dest], sib
        )

    for i in range(CHIPS):
        for a in range(3):
            sib_copy(a, i).start()
    w_copies = []
    for w in range(3):
        for k, p in enumerate(peers):
            cp = remote(shard_of(wp[w], p), wrecv[w].at[k], w_s.at[w, k], w_r.at[w, k], (p, e))
            cp.start()
            w_copies.append(cp)

    def wait_sib(a, dest):
        remote(
            srecv[a].at[dest], srecv[a].at[dest], sib_s.at[a, dest], sib_r.at[a, dest], sib
        ).wait_recv()

    def wait_line(a, dr, dest):
        ref = lrecv[a].at[dr, dest]
        remote(ref, ref, line_s.at[a, dr, dest], line_r.at[a, dr, dest], sib).wait_recv()

    def line_copy(a, dr, dest):
        return remote(
            srecv[a].at[dest],
            lrecv[a].at[dr, dest],
            line_s.at[a, dr, dest],
            line_r.at[a, dr, dest],
            (q, e + 2 if dr == 0 else e - 2),
        )

    def add_into(out, terms):
        rows = out.shape[0]
        step = min(rows, 16)

        @pl.loop(0, rows // step)
        def _(i):
            at = pl.ds(pl.multiple_of(i * step, step), step)
            total = terms[0][at, :].astype(jnp.float32)
            for t in terms[1:]:
                total = total + t[at, :].astype(jnp.float32)
            out[at, :] = total.astype(out.dtype)

    for i in range(CHIPS - 1):
        for a in range(3):
            for dr in range(2):
                dest = CHIPS - 1 - i if dr == 0 else i
                inner = z > 0 if dr == 0 else z < CHIPS - 1

                @pl.when(dest > z if dr == 0 else dest < z)
                def _():
                    wait_sib(a, dest)
                    mine, held = parts[a].at[2 * dest + c], srecv[a].at[dest]

                    @pl.when(inner)
                    def _():
                        wait_line(a, dr, dest)
                        add_into(held, (mine, held, lrecv[a].at[dr, dest]))

                    @pl.when(jnp.logical_not(inner))
                    def _():
                        add_into(held, (mine, held))

                    line_copy(a, dr, dest).start()

    for w in range(3):
        for k in range(3):
            w_copies[3 * w + k].wait_recv()
        add_into(wout[w], (shard_of(wp[w], q),) + tuple(wrecv[w].at[k] for k in range(3)))

    for a in range(3):
        wait_sib(a, z)
        mine, other = parts[a].at[2 * z + c], srecv[a].at[z]

        @pl.when(z == 0)
        def _():
            wait_line(a, 1, z)
            add_into(outs[a], (mine, other, lrecv[a].at[1, z]))

        @pl.when(z == CHIPS - 1)
        def _():
            wait_line(a, 0, z)
            add_into(outs[a], (mine, other, lrecv[a].at[0, z]))

        @pl.when(jnp.logical_and(z > 0, z < CHIPS - 1))
        def _():
            wait_line(a, 0, z)
            wait_line(a, 1, z)
            add_into(outs[a], (mine, other, lrecv[a].at[0, z], lrecv[a].at[1, z]))

    for cp in w_copies:
        cp.wait_send()
    for i in range(CHIPS):
        for a in range(3):
            sib_copy(a, i).wait_send()
    for a in range(3):
        for i in range(CHIPS - 1):
            for dr in range(2):
                dest = CHIPS - 1 - i if dr == 0 else i
                pl.when(dest > z if dr == 0 else dest < z)(
                    lambda: line_copy(a, dr, dest).wait_send()
                )


def reduce_all(parts, weight_parts):
    n, rows, width = parts[0].shape
    dma = pltpu.SemaphoreType.DMA
    vmem = pl.BlockSpec(memory_space=pltpu.VMEM)
    depth, hid = weight_parts[0].shape[1:]
    shards = [(depth, hid), (depth, hid), (hid, depth)]
    return pl.pallas_call(
        reduce_kernel,
        out_shape=tuple(jax.ShapeDtypeStruct(p.shape[1:], p.dtype) for p in parts)
        + tuple(jax.ShapeDtypeStruct(s, jnp.float32) for s in shards),
        in_specs=[vmem] * 6,
        out_specs=(vmem,) * 6,
        scratch_shapes=[pltpu.VMEM((CHIPS,) + p.shape[1:], p.dtype) for p in parts]
        + [pltpu.VMEM((2, CHIPS) + p.shape[1:], p.dtype) for p in parts]
        + [pltpu.VMEM((3,) + s, jnp.bfloat16) for s in shards]
        + [dma((3, 4)), dma((3, 4)), dma((3, 2, 4)), dma((3, 2, 4)), dma((3, 3)), dma((3, 3))],
        compiler_params=pltpu.CompilerParams(
            collective_id=1, has_side_effects=True, vmem_limit_bytes=56 << 20
        ),
    )(*parts, *weight_parts)


def on_device(tokens, cotangent, expert_ids, gate_probs, w_gate, w_up, w_down):
    n = lax.axis_size("expert")
    rows, width = tokens.shape
    f32, bf16 = jnp.float32, jnp.bfloat16
    me = lax.axis_index("expert")
    named = expert_ids[None, :, :] == jnp.arange(n, dtype=jnp.int32)[:, None, None]
    weights_t = jnp.sum(jnp.where(named, gate_probs.astype(f32)[None], 0.0), axis=2)
    toks, cots, gates, full_gate, full_up, full_down = gather_all(
        tokens, cotangent, weights_t, w_gate[0], w_up[0], w_down[0]
    )
    x = toks.reshape(n * rows, width)
    cot = cots.reshape(n * rows, width)
    wg = full_gate.reshape(width, -1)
    wu = full_up.reshape(width, -1)
    g = lax.dynamic_index_in_dim(gates, me, axis=1, keepdims=False).reshape(n * rows, 1)
    dot = functools.partial(lax.dot_general, preferred_element_type=f32)
    mm, nt, tn = (((1,), (0,)), ((), ())), (((1,), (1,)), ((), ())), (((0,), (0,)), ((), ()))
    pre_gate = dot(x, wg, mm)
    pre_up = dot(x, wu, mm)
    back = dot(cot, full_down, nt)
    activated, slope = silu_parts(pre_gate)
    hidden = activated * pre_up
    weighted = (g * hidden).astype(bf16)
    gate_grad = jnp.sum(hidden * back, axis=1)
    grad_hidden = g * back
    grad_pre_gate = (grad_hidden * pre_up * slope).astype(bf16)
    grad_pre_up = (grad_hidden * activated).astype(bf16)
    part_mixed = dot(weighted, full_down, mm).astype(bf16).reshape(n, rows, width)
    part_tokens = (dot(grad_pre_gate, wg, nt) + dot(grad_pre_up, wu, nt)).astype(bf16)
    part_tokens = part_tokens.reshape(n, rows, width)
    part_gates = jnp.where(
        (jnp.arange(n) == me)[None, :, None], gate_grad.reshape(n, 1, rows), 0.0
    )
    part_gate_w = dot(x, grad_pre_gate, tn).astype(bf16).reshape(full_gate.shape)
    part_up_w = dot(x, grad_pre_up, tn).astype(bf16).reshape(full_up.shape)
    part_down_w = dot(weighted, cot, tn).astype(bf16)
    mixed, grad_tokens, gates_all, gw, uw, dw = reduce_all(
        (part_mixed, part_tokens, part_gates), (part_gate_w, part_up_w, part_down_w)
    )
    grad_gates = jnp.sum(jnp.where(named, gates_all[:, :, None], 0.0), axis=0)
    return (mixed, grad_tokens, grad_gates, gw[None], uw[None], dw[None])


def solution(mesh):
    small = mesh.shape["expert"] == 2 * CHIPS and mesh.shape["dp"] == 4
    in_specs = (
        P(("dp", "expert"), None),
        P(("dp", "expert"), None),
        P(("dp", "expert"), None),
        P(("dp", "expert"), None),
        P("expert", "dp", None),
        P("expert", "dp", None),
        P("expert", None, "dp"),
    )
    out_specs = (
        P(("dp", "expert"), None),
        P(("dp", "expert"), None),
        P(("dp", "expert"), None),
        P("expert", "dp", None),
        P("expert", "dp", None),
        P("expert", None, "dp"),
    )
    return jax.shard_map(
        on_device if small else on_device_routed,
        mesh=mesh,
        in_specs=in_specs,
        out_specs=out_specs,
        check_vma=False,
    )
```

```python
import functools

import jax
import jax.numpy as jnp
from jax import lax
from jax.experimental import pallas as pl
from jax.experimental.pallas import tpu as pltpu
from jax.sharding import PartitionSpec as P


def silu_parts(pre_gate):
    sigma = jax.nn.sigmoid(pre_gate)
    return (pre_gate * sigma, sigma * (1.0 + pre_gate * (1.0 - sigma)))


def on_device_routed(tokens, cotangent, expert_ids, gate_probs, w_gate, w_up, w_down):
    axis_count = lax.axis_size("expert")
    local_experts = w_gate.shape[0]
    tok_rows = tokens.shape[0]
    model_width = tokens.shape[1]
    top_count = expert_ids.shape[1]
    all_experts = local_experts * axis_count
    capacity = max(2, 5 * tok_rows * top_count // (4 * all_experts))
    pair_count = tok_rows * top_count
    flat_ids = expert_ids.reshape(-1)
    onehot = (flat_ids[:, None] == jnp.arange(all_experts, dtype=jnp.int32)[None, :]).astype(
        jnp.int32
    )
    before = jnp.tril(jnp.ones((pair_count, pair_count), jnp.bfloat16), -1)
    earlier = jnp.dot(
        before, onehot.astype(jnp.bfloat16), preferred_element_type=jnp.float32
    ).astype(jnp.int32)
    slot_rank = jnp.sum(earlier * onehot, axis=1)
    position = flat_ids * capacity + slot_rank
    pair_table = jnp.full((all_experts * capacity,), pair_count, jnp.int32)
    pair_table = pair_table.at[position].set(jnp.arange(pair_count, dtype=jnp.int32))
    routed = (
        gate_probs.astype(jnp.float32)[:, :, None] * cotangent.astype(jnp.float32)[:, None, :]
    ).astype(jnp.bfloat16)
    routed = routed.reshape(pair_count, model_width)
    send_shape = (axis_count, local_experts, capacity, model_width)
    token_send = jnp.take(
        tokens, pair_table // top_count, axis=0, mode="fill", fill_value=0
    ).reshape(send_shape)
    routed_send = jnp.take(routed, pair_table, axis=0, mode="fill", fill_value=0).reshape(
        send_shape
    )
    token_recv, routed_recv = (
        lax.all_to_all(token_send, "expert", split_axis=0, concat_axis=2, tiled=True),
        lax.all_to_all(routed_send, "expert", split_axis=0, concat_axis=2, tiled=True),
    )
    rows_in = token_recv[0]
    routed_in = routed_recv[0]
    full_gate, full_up, full_down = (
        lax.all_gather(w_gate, "dp", axis=1, tiled=True),
        lax.all_gather(w_up, "dp", axis=1, tiled=True),
        lax.all_gather(w_down, "dp", axis=2, tiled=True),
    )
    pre_gate = jnp.einsum("end,edf->enf", rows_in, full_gate, preferred_element_type=jnp.float32)
    pre_up = jnp.einsum("end,edf->enf", rows_in, full_up, preferred_element_type=jnp.float32)
    activated, slope = silu_parts(pre_gate)
    hidden = (activated * pre_up).astype(jnp.bfloat16)
    expert_out = jnp.einsum(
        "enf,efd->end", hidden, full_down, preferred_element_type=jnp.float32
    ).astype(jnp.bfloat16)
    grad_hidden = jnp.einsum(
        "end,efd->enf", routed_in, full_down, preferred_element_type=jnp.float32
    )
    grad_pre_gate = (grad_hidden * pre_up * slope).astype(jnp.bfloat16)
    grad_pre_up = (grad_hidden * activated).astype(jnp.bfloat16)
    pair_grad = jnp.einsum(
        "enf,edf->end", grad_pre_gate, full_gate, preferred_element_type=jnp.float32
    )
    pair_grad = pair_grad + jnp.einsum(
        "enf,edf->end", grad_pre_up, full_up, preferred_element_type=jnp.float32
    )
    pair_grad = pair_grad.astype(jnp.bfloat16)
    back_out, back_grad = (
        lax.all_to_all(expert_out[None], "expert", split_axis=2, concat_axis=0, tiled=True),
        lax.all_to_all(pair_grad[None], "expert", split_axis=2, concat_axis=0, tiled=True),
    )
    out_pairs = back_out.reshape(all_experts * capacity, model_width)[position].reshape(
        tok_rows, top_count, model_width
    )
    grad_pairs = back_grad.reshape(all_experts * capacity, model_width)[position].reshape(
        tok_rows, top_count, model_width
    )
    mixed = jnp.einsum(
        "tk,tkd->td", gate_probs, out_pairs, preferred_element_type=jnp.float32
    ).astype(jnp.bfloat16)
    grad_gates = jnp.einsum("td,tkd->tk", cotangent, out_pairs, preferred_element_type=jnp.float32)
    grad_tokens = jnp.sum(grad_pairs.astype(jnp.float32), axis=1).astype(jnp.bfloat16)
    part_gate = jnp.einsum(
        "end,enf->edf", rows_in, grad_pre_gate, preferred_element_type=jnp.float32
    )
    part_up = jnp.einsum("end,enf->edf", rows_in, grad_pre_up, preferred_element_type=jnp.float32)
    part_down = jnp.einsum("enf,end->efd", hidden, routed_in, preferred_element_type=jnp.float32)
    grad_gate_w, grad_up_w, grad_down_w = (
        lax.psum_scatter(
            part_gate.astype(jnp.bfloat16), "dp", scatter_dimension=1, tiled=True
        ).astype(jnp.float32),
        lax.psum_scatter(
            part_up.astype(jnp.bfloat16), "dp", scatter_dimension=1, tiled=True
        ).astype(jnp.float32),
        lax.psum_scatter(
            part_down.astype(jnp.bfloat16), "dp", scatter_dimension=2, tiled=True
        ).astype(jnp.float32),
    )
    return (mixed, grad_tokens, grad_gates, grad_gate_w, grad_up_w, grad_down_w)


MESH = pl.DeviceIdType.MESH
CHIPS = 4


def places():
    q, e = lax.axis_index("dp"), lax.axis_index("expert")
    z, c = e // 2, e % 2
    x, y = q % 2, q // 2
    xn, yn, dn = 2 * y + 1 - x, 2 * (1 - y) + x, 2 * (1 - y) + 1 - x
    return q, e, z, c, xn, yn, dn


def greet(q, e, z, c, dp_peers):
    barrier = pltpu.get_barrier_semaphore()

    def hello(dev):
        pl.semaphore_signal(barrier, inc=1, device_id=dev, device_id_type=MESH)

    pl.when(z > 0)(lambda: hello((q, e - 2)))
    pl.when(z < CHIPS - 1)(lambda: hello((q, e + 2)))
    hello((q, 2 * z + 1 - c))
    for p in dp_peers:
        hello((p, e))
    line = jnp.where(z > 0, 1, 0) + jnp.where(z < CHIPS - 1, 1, 0)
    pl.semaphore_wait(barrier, line + (1 + len(dp_peers)))


def remote(src, dst, send, recv, dev):
    return pltpu.make_async_remote_copy(
        src_ref=src, dst_ref=dst, send_sem=send, recv_sem=recv, device_id=dev, device_id_type=MESH
    )


def shard_of(ref, q, start=0, rows=None):
    rows = ref.shape[-2] if rows is None else rows
    if len(ref.shape) == 3:
        return ref.at[q, pl.ds(start, rows)]
    width = ref.shape[1] // 4
    return ref.at[pl.ds(start, rows), pl.ds(pl.multiple_of(q * width, 128), width)]


def gather_kernel(*refs):
    ins, ws = refs[0:3], refs[3:6]
    alls, wall = refs[6:9], refs[9:12]
    own_sem, w_own, line_s, line_r, sib_s, sib_r, ws_s, ws_r = refs[12:]
    q, e, z, c, xn, yn, dn = places()
    sib = (q, 2 * z + 1 - c)
    greet(q, e, z, c, (xn, yn))

    half = ws[0].shape[0] // 2
    w_sends = []
    for w in range(3):
        for k, p in enumerate((xn, yn)):
            cp = remote(ws[w], shard_of(wall[w], q), ws_s.at[w, k], ws_r.at[w, k], (p, e))
            cp.start()
            w_sends.append(cp)

    def block(a, zs, core):
        return alls[a].at[2 * zs + core]

    def source(a, zs, d):
        return ins[a] if d == 0 else block(a, zs, c)

    def line_copy(a, dr, d):
        zs, to = (z - d, e + 2) if dr == 0 else (z + d, e - 2)
        return remote(
            source(a, zs, d), block(a, zs, c), line_s.at[a, dr, d], line_r.at[a, dr, d], (q, to)
        )

    def sib_copy(a, dr, d):
        zs = z - d if dr == 0 else z + d
        return remote(source(a, zs, d), block(a, zs, c), sib_s.at[a, dr, d], sib_r.at[a, dr, d], sib)

    def has_block(dr, d):
        return z - d >= 0 if dr == 0 else z + d <= CHIPS - 1

    def forwards(dr, d):
        return (
            jnp.logical_and(z - d >= 0, z < CHIPS - 1)
            if dr == 0
            else jnp.logical_and(z + d <= CHIPS - 1, z > 0)
        )

    locals_ = []
    for d in range(CHIPS):
        for a in range(3):
            for dr in range(2):
                if d > 0:

                    @pl.when(has_block(dr, d))
                    def _():
                        zs = z - d if dr == 0 else z + d
                        remote(
                            block(a, zs, c),
                            block(a, zs, c),
                            line_s.at[a, dr, d - 1],
                            line_r.at[a, dr, d - 1],
                            sib,
                        ).wait_recv()

                if d < CHIPS - 1:
                    pl.when(forwards(dr, d))(lambda: line_copy(a, dr, d).start())
                if d > 0:
                    pl.when(has_block(dr, d))(lambda: sib_copy(a, dr, d).start())
                elif dr == 0:
                    sib_copy(a, 0, 0).start()
        if d == 0:
            for a in range(3):
                cp = pltpu.make_async_copy(ins[a], alls[a].at[e], own_sem.at[a])
                cp.start()
                locals_.append(cp)
            for w in range(3):
                cp = pltpu.make_async_copy(ws[w], shard_of(wall[w], q), w_own.at[w])
                cp.start()
                locals_.append(cp)
        if d == 1:
            for w in range(3):
                for k, (p, other) in enumerate(((xn, yn), (yn, xn))):
                    whole = shard_of(wall[w], p)
                    remote(whole, whole, ws_s.at[w, k], ws_r.at[w, k], (p, e)).wait_recv()
                    part = shard_of(wall[w], p, half * k, half)
                    cp = remote(part, part, ws_s.at[w, 2 + k], ws_r.at[w, 2 + k], (other, e))
                    cp.start()
                    w_sends.append(cp)
    for cp in locals_:
        cp.wait()
    for w in range(3):
        for k in range(2):
            part = shard_of(wall[w], dn, half * k, half)
            remote(part, part, ws_s.at[w, 2 + k], ws_r.at[w, 2 + k], (xn, e)).wait_recv()
    for cp in w_sends:
        cp.wait_send()
    for d in range(CHIPS):
        for a in range(3):
            for dr in range(2):
                if d < CHIPS - 1:
                    pl.when(forwards(dr, d))(lambda: line_copy(a, dr, d).wait_send())
                if d == 0 and dr == 1:
                    continue

                @pl.when(has_block(dr, d))
                def _():
                    zs = z - d if dr == 0 else z + d
                    sib_copy(a, dr, d).wait_send()
                    got = block(a, zs, 1 - c)
                    remote(got, got, sib_s.at[a, dr, d], sib_r.at[a, dr, d], sib).wait_recv()


def gather_all(tokens, cotangent, weights_t, w_gate, w_up, w_down):
    rows, width = tokens.shape
    n = weights_t.shape[0]
    depth, hid = w_gate.shape
    any_ = pl.BlockSpec(memory_space=pl.ANY)
    dma = pltpu.SemaphoreType.DMA
    return pl.pallas_call(
        gather_kernel,
        out_shape=(
            jax.ShapeDtypeStruct((n, rows, width), tokens.dtype),
            jax.ShapeDtypeStruct((n, rows, width), tokens.dtype),
            jax.ShapeDtypeStruct((n,) + weights_t.shape, weights_t.dtype),
            jax.ShapeDtypeStruct((4, depth, hid), w_gate.dtype),
            jax.ShapeDtypeStruct((4, depth, hid), w_gate.dtype),
            jax.ShapeDtypeStruct((hid, 4 * depth), w_gate.dtype),
        ),
        in_specs=[any_] * 6,
        out_specs=(any_,) * 6,
        scratch_shapes=[
            dma((3,)),
            dma((3,)),
            dma((3, 2, 3)),
            dma((3, 2, 3)),
            dma((3, 2, 4)),
            dma((3, 2, 4)),
            dma((3, 4)),
            dma((3, 4)),
        ],
        compiler_params=pltpu.CompilerParams(collective_id=0, has_side_effects=True),
    )(tokens, cotangent, weights_t, w_gate, w_up, w_down)


def reduce_kernel(*refs):
    parts, wp = refs[0:3], refs[3:6]
    outs, wout = refs[6:9], refs[9:12]
    srecv, lrecv, wrecv = refs[12:15], refs[15:18], refs[18:21]
    sib_s, sib_r, line_s, line_r, w_s, w_r = refs[21:]
    q, e, z, c, xn, yn, dn = places()
    sib = (q, 2 * z + 1 - c)
    greet(q, e, z, c, (xn, yn))

    def sib_copy(a, i):
        dest = CHIPS - 1 - i // 2 if i % 2 == 0 else i // 2
        return remote(
            parts[a].at[2 * dest + 1 - c], srecv[a].at[dest], sib_s.at[a, dest], sib_r.at[a, dest], sib
        )

    def start_sib(a, pair):
        sib_copy(a, 2 * pair).start()
        sib_copy(a, 2 * pair + 1).start()

    half = wout[0].shape[0] // 2
    w_copies = []

    def w_send(w, slot, src, p):
        cp = remote(src, wrecv[w].at[slot], w_s.at[w, slot], w_r.at[w, slot], (p, e))
        cp.start()
        w_copies.append(cp)

    def w_got(w, slot):
        ref = wrecv[w].at[slot]
        remote(ref, ref, w_s.at[w, slot], w_r.at[w, slot], (xn, e)).wait_recv()
        return ref

    start_sib(0, 0)

    def wait_sib(a, dest):
        remote(
            srecv[a].at[dest], srecv[a].at[dest], sib_s.at[a, dest], sib_r.at[a, dest], sib
        ).wait_recv()

    def wait_line(a, dr, dest):
        ref = lrecv[a].at[dr, dest]
        remote(ref, ref, line_s.at[a, dr, dest], line_r.at[a, dr, dest], sib).wait_recv()

    def line_copy(a, dr, dest):
        return remote(
            srecv[a].at[dest],
            lrecv[a].at[dr, dest],
            line_s.at[a, dr, dest],
            line_r.at[a, dr, dest],
            (q, e + 2 if dr == 0 else e - 2),
        )

    def add_into(out, terms):
        rows = out.shape[0]
        step = min(rows, 16)

        @pl.loop(0, rows // step)
        def _(i):
            at = pl.ds(pl.multiple_of(i * step, step), step)
            total = terms[0][at, :].astype(jnp.float32)
            for t in terms[1:]:
                total = total + t[at, :].astype(jnp.float32)
            out[at, :] = total.astype(out.dtype)

    for i in range(CHIPS - 1):
        for a in range(3):
            for dr in range(2):
                if i == 0 and dr == 0:
                    if a == 0:
                        start_sib(1, 0)
                        start_sib(2, 0)
                        for w in range(3):
                            w_send(w, 1, shard_of(wp[w], dn, 0, half), xn)
                            w_send(w, 3, shard_of(wp[w], dn, half, half), yn)
                            w_send(w, 0, shard_of(wp[w], xn, 0, half), xn)
                            w_send(w, 2, shard_of(wp[w], yn, half, half), yn)
                    elif a == 1:
                        start_sib(0, 1)
                    else:
                        start_sib(1, 1)
                        start_sib(2, 1)
                dest = CHIPS - 1 - i if dr == 0 else i
                inner = z > 0 if dr == 0 else z < CHIPS - 1

                @pl.when(dest > z if dr == 0 else dest < z)
                def _():
                    wait_sib(a, dest)
                    mine, held = parts[a].at[2 * dest + c], srecv[a].at[dest]

                    @pl.when(inner)
                    def _():
                        wait_line(a, dr, dest)
                        add_into(held, (mine, held, lrecv[a].at[dr, dest]))

                    @pl.when(jnp.logical_not(inner))
                    def _():
                        add_into(held, (mine, held))

                    line_copy(a, dr, dest).start()

        if i == 0:
            for w in range(3):
                held = wrecv[w].at[6]
                add_into(held, (shard_of(wp[w], yn, 0, half), w_got(w, 1)))
                w_send(w, 4, held, yn)
                held = wrecv[w].at[7]
                add_into(held, (shard_of(wp[w], xn, half, half), w_got(w, 3)))
                w_send(w, 5, held, xn)

    for w in range(3):
        for k in range(2):
            terms = (shard_of(wp[w], q, half * k, half), w_got(w, 2 * k), w_got(w, 4 + k))
            add_into(wout[w].at[pl.ds(half * k, half)], terms)

    for a in range(3):
        wait_sib(a, z)
        mine, other = parts[a].at[2 * z + c], srecv[a].at[z]

        @pl.when(z == 0)
        def _():
            wait_line(a, 1, z)
            add_into(outs[a], (mine, other, lrecv[a].at[1, z]))

        @pl.when(z == CHIPS - 1)
        def _():
            wait_line(a, 0, z)
            add_into(outs[a], (mine, other, lrecv[a].at[0, z]))

        @pl.when(jnp.logical_and(z > 0, z < CHIPS - 1))
        def _():
            wait_line(a, 0, z)
            wait_line(a, 1, z)
            add_into(outs[a], (mine, other, lrecv[a].at[0, z], lrecv[a].at[1, z]))

    for cp in w_copies:
        cp.wait_send()
    for i in range(CHIPS):
        for a in range(3):
            sib_copy(a, i).wait_send()
    for a in range(3):
        for i in range(CHIPS - 1):
            for dr in range(2):
                dest = CHIPS - 1 - i if dr == 0 else i
                pl.when(dest > z if dr == 0 else dest < z)(
                    lambda: line_copy(a, dr, dest).wait_send()
                )


def reduce_all(parts, weight_parts):
    n, rows, width = parts[0].shape
    dma = pltpu.SemaphoreType.DMA
    vmem = pl.BlockSpec(memory_space=pltpu.VMEM)
    depth, hid = weight_parts[0].shape[1:]
    shards = [(depth, hid), (depth, hid), (hid, depth)]
    return pl.pallas_call(
        reduce_kernel,
        out_shape=tuple(jax.ShapeDtypeStruct(p.shape[1:], p.dtype) for p in parts)
        + tuple(jax.ShapeDtypeStruct(s, jnp.float32) for s in shards),
        in_specs=[vmem] * 6,
        out_specs=(vmem,) * 6,
        scratch_shapes=[pltpu.VMEM((CHIPS,) + p.shape[1:], p.dtype) for p in parts]
        + [pltpu.VMEM((2, CHIPS) + p.shape[1:], p.dtype) for p in parts]
        + [pltpu.VMEM((8, s[0] // 2, s[1]), jnp.bfloat16) for s in shards]
        + [dma((3, 4)), dma((3, 4)), dma((3, 2, 4)), dma((3, 2, 4)), dma((3, 6)), dma((3, 6))],
        compiler_params=pltpu.CompilerParams(
            collective_id=1, has_side_effects=True, vmem_limit_bytes=56 << 20
        ),
    )(*parts, *weight_parts)


def on_device(tokens, cotangent, expert_ids, gate_probs, w_gate, w_up, w_down):
    n = lax.axis_size("expert")
    rows, width = tokens.shape
    f32, bf16 = jnp.float32, jnp.bfloat16
    me = lax.axis_index("expert")
    named = expert_ids[None, :, :] == jnp.arange(n, dtype=jnp.int32)[:, None, None]
    weights_t = jnp.sum(jnp.where(named, gate_probs.astype(f32)[None], 0.0), axis=2)
    toks, cots, gates, full_gate, full_up, full_down = gather_all(
        tokens, cotangent, weights_t, w_gate[0], w_up[0], w_down[0]
    )
    x = toks.reshape(n * rows, width)
    cot = cots.reshape(n * rows, width)
    wg = full_gate.reshape(width, -1)
    wu = full_up.reshape(width, -1)
    g = lax.dynamic_index_in_dim(gates, me, axis=1, keepdims=False).reshape(n * rows, 1)
    dot = functools.partial(lax.dot_general, preferred_element_type=f32)
    mm, nt, tn = (((1,), (0,)), ((), ())), (((1,), (1,)), ((), ())), (((0,), (0,)), ((), ()))
    pre_gate = dot(x, wg, mm)
    pre_up = dot(x, wu, mm)
    back = dot(cot, full_down, nt)
    activated, slope = silu_parts(pre_gate)
    hidden = activated * pre_up
    weighted = (g * hidden).astype(bf16)
    gate_grad = jnp.sum(hidden * back, axis=1)
    grad_hidden = g * back
    grad_pre_gate = (grad_hidden * pre_up * slope).astype(bf16)
    grad_pre_up = (grad_hidden * activated).astype(bf16)
    part_mixed = dot(weighted, full_down, mm).astype(bf16).reshape(n, rows, width)
    part_tokens = (dot(grad_pre_gate, wg, nt) + dot(grad_pre_up, wu, nt)).astype(bf16)
    part_tokens = part_tokens.reshape(n, rows, width)
    part_gates = jnp.where(
        (jnp.arange(n) == me)[None, :, None], gate_grad.reshape(n, 1, rows), 0.0
    )
    part_gate_w = dot(x, grad_pre_gate, tn).astype(bf16).reshape(full_gate.shape)
    part_up_w = dot(x, grad_pre_up, tn).astype(bf16).reshape(full_up.shape)
    part_down_w = dot(weighted, cot, tn).astype(bf16)
    mixed, grad_tokens, gates_all, gw, uw, dw = reduce_all(
        (part_mixed, part_tokens, part_gates), (part_gate_w, part_up_w, part_down_w)
    )
    grad_gates = jnp.sum(jnp.where(named, gates_all[:, :, None], 0.0), axis=0)
    return (mixed, grad_tokens, grad_gates, gw[None], uw[None], dw[None])


def solution(mesh):
    small = mesh.shape["expert"] == 2 * CHIPS and mesh.shape["dp"] == 4
    in_specs = (
        P(("dp", "expert"), None),
        P(("dp", "expert"), None),
        P(("dp", "expert"), None),
        P(("dp", "expert"), None),
        P("expert", "dp", None),
        P("expert", "dp", None),
        P("expert", None, "dp"),
    )
    out_specs = (
        P(("dp", "expert"), None),
        P(("dp", "expert"), None),
        P(("dp", "expert"), None),
        P("expert", "dp", None),
        P("expert", "dp", None),
        P("expert", None, "dp"),
    )
    return jax.shard_map(
        on_device if small else on_device_routed,
        mesh=mesh,
        in_specs=in_specs,
        out_specs=out_specs,
        check_vma=False,
    )
```

```python
import functools

import jax
import jax.numpy as jnp
from jax import lax
from jax.experimental import pallas as pl
from jax.experimental.pallas import tpu as pltpu
from jax.sharding import PartitionSpec as P


def silu_parts(pre_gate):
    sigma = jax.nn.sigmoid(pre_gate)
    return (pre_gate * sigma, sigma * (1.0 + pre_gate * (1.0 - sigma)))


def on_device_routed(tokens, cotangent, expert_ids, gate_probs, w_gate, w_up, w_down):
    axis_count = lax.axis_size("expert")
    local_experts = w_gate.shape[0]
    tok_rows = tokens.shape[0]
    model_width = tokens.shape[1]
    top_count = expert_ids.shape[1]
    all_experts = local_experts * axis_count
    capacity = max(2, 5 * tok_rows * top_count // (4 * all_experts))
    pair_count = tok_rows * top_count
    flat_ids = expert_ids.reshape(-1)
    onehot = (flat_ids[:, None] == jnp.arange(all_experts, dtype=jnp.int32)[None, :]).astype(
        jnp.int32
    )
    before = jnp.tril(jnp.ones((pair_count, pair_count), jnp.bfloat16), -1)
    earlier = jnp.dot(
        before, onehot.astype(jnp.bfloat16), preferred_element_type=jnp.float32
    ).astype(jnp.int32)
    slot_rank = jnp.sum(earlier * onehot, axis=1)
    position = flat_ids * capacity + slot_rank
    pair_table = jnp.full((all_experts * capacity,), pair_count, jnp.int32)
    pair_table = pair_table.at[position].set(jnp.arange(pair_count, dtype=jnp.int32))
    routed = (
        gate_probs.astype(jnp.float32)[:, :, None] * cotangent.astype(jnp.float32)[:, None, :]
    ).astype(jnp.bfloat16)
    routed = routed.reshape(pair_count, model_width)
    send_shape = (axis_count, local_experts, capacity, model_width)
    token_send = jnp.take(
        tokens, pair_table // top_count, axis=0, mode="fill", fill_value=0
    ).reshape(send_shape)
    routed_send = jnp.take(routed, pair_table, axis=0, mode="fill", fill_value=0).reshape(
        send_shape
    )
    token_recv, routed_recv = (
        lax.all_to_all(token_send, "expert", split_axis=0, concat_axis=2, tiled=True),
        lax.all_to_all(routed_send, "expert", split_axis=0, concat_axis=2, tiled=True),
    )
    rows_in = token_recv[0]
    routed_in = routed_recv[0]
    full_gate, full_up, full_down = (
        lax.all_gather(w_gate, "dp", axis=1, tiled=True),
        lax.all_gather(w_up, "dp", axis=1, tiled=True),
        lax.all_gather(w_down, "dp", axis=2, tiled=True),
    )
    pre_gate = jnp.einsum("end,edf->enf", rows_in, full_gate, preferred_element_type=jnp.float32)
    pre_up = jnp.einsum("end,edf->enf", rows_in, full_up, preferred_element_type=jnp.float32)
    activated, slope = silu_parts(pre_gate)
    hidden = (activated * pre_up).astype(jnp.bfloat16)
    expert_out = jnp.einsum(
        "enf,efd->end", hidden, full_down, preferred_element_type=jnp.float32
    ).astype(jnp.bfloat16)
    grad_hidden = jnp.einsum(
        "end,efd->enf", routed_in, full_down, preferred_element_type=jnp.float32
    )
    grad_pre_gate = (grad_hidden * pre_up * slope).astype(jnp.bfloat16)
    grad_pre_up = (grad_hidden * activated).astype(jnp.bfloat16)
    pair_grad = jnp.einsum(
        "enf,edf->end", grad_pre_gate, full_gate, preferred_element_type=jnp.float32
    )
    pair_grad = pair_grad + jnp.einsum(
        "enf,edf->end", grad_pre_up, full_up, preferred_element_type=jnp.float32
    )
    pair_grad = pair_grad.astype(jnp.bfloat16)
    back_out, back_grad = (
        lax.all_to_all(expert_out[None], "expert", split_axis=2, concat_axis=0, tiled=True),
        lax.all_to_all(pair_grad[None], "expert", split_axis=2, concat_axis=0, tiled=True),
    )
    out_pairs = back_out.reshape(all_experts * capacity, model_width)[position].reshape(
        tok_rows, top_count, model_width
    )
    grad_pairs = back_grad.reshape(all_experts * capacity, model_width)[position].reshape(
        tok_rows, top_count, model_width
    )
    mixed = jnp.einsum(
        "tk,tkd->td", gate_probs, out_pairs, preferred_element_type=jnp.float32
    ).astype(jnp.bfloat16)
    grad_gates = jnp.einsum("td,tkd->tk", cotangent, out_pairs, preferred_element_type=jnp.float32)
    grad_tokens = jnp.sum(grad_pairs.astype(jnp.float32), axis=1).astype(jnp.bfloat16)
    part_gate = jnp.einsum(
        "end,enf->edf", rows_in, grad_pre_gate, preferred_element_type=jnp.float32
    )
    part_up = jnp.einsum("end,enf->edf", rows_in, grad_pre_up, preferred_element_type=jnp.float32)
    part_down = jnp.einsum("enf,end->efd", hidden, routed_in, preferred_element_type=jnp.float32)
    grad_gate_w, grad_up_w, grad_down_w = (
        lax.psum_scatter(
            part_gate.astype(jnp.bfloat16), "dp", scatter_dimension=1, tiled=True
        ).astype(jnp.float32),
        lax.psum_scatter(
            part_up.astype(jnp.bfloat16), "dp", scatter_dimension=1, tiled=True
        ).astype(jnp.float32),
        lax.psum_scatter(
            part_down.astype(jnp.bfloat16), "dp", scatter_dimension=2, tiled=True
        ).astype(jnp.float32),
    )
    return (mixed, grad_tokens, grad_gates, grad_gate_w, grad_up_w, grad_down_w)


MESH = pl.DeviceIdType.MESH
CHIPS = 4


def places():
    q, e = lax.axis_index("dp"), lax.axis_index("expert")
    z, c = e // 2, e % 2
    x, y = q % 2, q // 2
    xn, yn, dn = 2 * y + 1 - x, 2 * (1 - y) + x, 2 * (1 - y) + 1 - x
    return q, e, z, c, xn, yn, dn


def greet(q, e, z, c, dp_peers):
    barrier = pltpu.get_barrier_semaphore()

    def hello(dev):
        pl.semaphore_signal(barrier, inc=1, device_id=dev, device_id_type=MESH)

    pl.when(z > 0)(lambda: hello((q, e - 2)))
    pl.when(z < CHIPS - 1)(lambda: hello((q, e + 2)))
    hello((q, 2 * z + 1 - c))
    for p in dp_peers:
        hello((p, e))
    line = jnp.where(z > 0, 1, 0) + jnp.where(z < CHIPS - 1, 1, 0)
    pl.semaphore_wait(barrier, line + (1 + len(dp_peers)))


def remote(src, dst, send, recv, dev):
    return pltpu.make_async_remote_copy(
        src_ref=src, dst_ref=dst, send_sem=send, recv_sem=recv, device_id=dev, device_id_type=MESH
    )


def shard_of(ref, q, start=0, rows=None):
    rows = ref.shape[-2] if rows is None else rows
    if len(ref.shape) == 3:
        return ref.at[q, pl.ds(start, rows)]
    width = ref.shape[1] // 4
    return ref.at[pl.ds(start, rows), pl.ds(pl.multiple_of(q * width, 128), width)]


def gather_kernel(*refs):
    ins, ws = refs[0:3], refs[3:6]
    alls, wall = refs[6:9], refs[9:12]
    own_sem, w_own, line_s, line_r, sib_s, sib_r, ws_s, ws_r = refs[12:]
    q, e, z, c, xn, yn, dn = places()
    sib = (q, 2 * z + 1 - c)
    greet(q, e, z, c, (xn, yn))

    half = ws[0].shape[0] // 2
    w_sends = []
    for w in range(3):
        for k, p in enumerate((xn, yn)):
            cp = remote(ws[w], shard_of(wall[w], q), ws_s.at[w, k], ws_r.at[w, k], (p, e))
            cp.start()
            w_sends.append(cp)

    def block(a, zs, core):
        return alls[a].at[2 * zs + core]

    def source(a, zs, d):
        return ins[a] if d == 0 else block(a, zs, c)

    def line_copy(a, dr, d):
        zs, to = (z - d, e + 2) if dr == 0 else (z + d, e - 2)
        return remote(
            source(a, zs, d), block(a, zs, c), line_s.at[a, dr, d], line_r.at[a, dr, d], (q, to)
        )

    def sib_copy(a, dr, d):
        zs = z - d if dr == 0 else z + d
        return remote(source(a, zs, d), block(a, zs, c), sib_s.at[a, dr, d], sib_r.at[a, dr, d], sib)

    def has_block(dr, d):
        return z - d >= 0 if dr == 0 else z + d <= CHIPS - 1

    def forwards(dr, d):
        return (
            jnp.logical_and(z - d >= 0, z < CHIPS - 1)
            if dr == 0
            else jnp.logical_and(z + d <= CHIPS - 1, z > 0)
        )

    locals_ = []
    for d in range(CHIPS):
        for a in range(3):
            for dr in range(2):
                if d > 0:

                    @pl.when(has_block(dr, d))
                    def _():
                        zs = z - d if dr == 0 else z + d
                        remote(
                            block(a, zs, c),
                            block(a, zs, c),
                            line_s.at[a, dr, d - 1],
                            line_r.at[a, dr, d - 1],
                            sib,
                        ).wait_recv()

                if d < CHIPS - 1:
                    pl.when(forwards(dr, d))(lambda: line_copy(a, dr, d).start())
                if d > 0:
                    pl.when(has_block(dr, d))(lambda: sib_copy(a, dr, d).start())
                elif dr == 0:
                    sib_copy(a, 0, 0).start()
        if d == 0:
            for a in range(3):
                cp = pltpu.make_async_copy(ins[a], alls[a].at[e], own_sem.at[a])
                cp.start()
                locals_.append(cp)
            for w in range(3):
                cp = pltpu.make_async_copy(ws[w], shard_of(wall[w], q), w_own.at[w])
                cp.start()
                locals_.append(cp)
        if d == 1:
            for w in range(3):
                for k, (p, other) in enumerate(((xn, yn), (yn, xn))):
                    whole = shard_of(wall[w], p)
                    remote(whole, whole, ws_s.at[w, k], ws_r.at[w, k], (p, e)).wait_recv()
                    part = shard_of(wall[w], p, half * k, half)
                    cp = remote(part, part, ws_s.at[w, 2 + k], ws_r.at[w, 2 + k], (other, e))
                    cp.start()
                    w_sends.append(cp)
    for cp in locals_:
        cp.wait()
    for w in range(3):
        for k in range(2):
            part = shard_of(wall[w], dn, half * k, half)
            remote(part, part, ws_s.at[w, 2 + k], ws_r.at[w, 2 + k], (xn, e)).wait_recv()
    for cp in w_sends:
        cp.wait_send()
    for d in range(CHIPS):
        for a in range(3):
            for dr in range(2):
                if d < CHIPS - 1:
                    pl.when(forwards(dr, d))(lambda: line_copy(a, dr, d).wait_send())
                if d == 0 and dr == 1:
                    continue

                @pl.when(has_block(dr, d))
                def _():
                    zs = z - d if dr == 0 else z + d
                    sib_copy(a, dr, d).wait_send()
                    got = block(a, zs, 1 - c)
                    remote(got, got, sib_s.at[a, dr, d], sib_r.at[a, dr, d], sib).wait_recv()


def gather_all(tokens, cotangent, weights_t, w_gate, w_up, w_down):
    rows, width = tokens.shape
    n = weights_t.shape[0]
    depth, hid = w_gate.shape
    any_ = pl.BlockSpec(memory_space=pl.ANY)
    dma = pltpu.SemaphoreType.DMA
    return pl.pallas_call(
        gather_kernel,
        out_shape=(
            jax.ShapeDtypeStruct((n, rows, width), tokens.dtype),
            jax.ShapeDtypeStruct((n, rows, width), tokens.dtype),
            jax.ShapeDtypeStruct((n,) + weights_t.shape, weights_t.dtype),
            jax.ShapeDtypeStruct((4, depth, hid), w_gate.dtype),
            jax.ShapeDtypeStruct((4, depth, hid), w_gate.dtype),
            jax.ShapeDtypeStruct((hid, 4 * depth), w_gate.dtype),
        ),
        in_specs=[any_] * 6,
        out_specs=(any_,) * 6,
        scratch_shapes=[
            dma((3,)),
            dma((3,)),
            dma((3, 2, 3)),
            dma((3, 2, 3)),
            dma((3, 2, 4)),
            dma((3, 2, 4)),
            dma((3, 4)),
            dma((3, 4)),
        ],
        compiler_params=pltpu.CompilerParams(collective_id=0, has_side_effects=True),
    )(tokens, cotangent, weights_t, w_gate, w_up, w_down)


def reduce_kernel(*refs):
    parts, wp = refs[0:3], refs[3:6]
    outs, wout = refs[6:9], refs[9:12]
    srecv, lrecv, wrecv = refs[12:15], refs[15:18], refs[18:21]
    sib_s, sib_r, line_s, line_r, w_s, w_r = refs[21:]
    q, e, z, c, xn, yn, dn = places()
    sib = (q, 2 * z + 1 - c)
    greet(q, e, z, c, (xn, yn))

    def sib_copy(a, i):
        dest = CHIPS - 1 - i // 2 if i % 2 == 0 else i // 2
        return remote(
            parts[a].at[2 * dest + 1 - c], srecv[a].at[dest], sib_s.at[a, dest], sib_r.at[a, dest], sib
        )

    def start_sib(a, pair):
        sib_copy(a, 2 * pair).start()
        sib_copy(a, 2 * pair + 1).start()

    half = wout[0].shape[0] // 2
    w_copies = []

    def w_send(w, slot, src, p):
        cp = remote(src, wrecv[w].at[slot], w_s.at[w, slot], w_r.at[w, slot], (p, e))
        cp.start()
        w_copies.append(cp)

    def w_got(w, slot):
        ref = wrecv[w].at[slot]
        remote(ref, ref, w_s.at[w, slot], w_r.at[w, slot], (xn, e)).wait_recv()
        return ref

    start_sib(0, 0)

    def wait_sib(a, dest):
        remote(
            srecv[a].at[dest], srecv[a].at[dest], sib_s.at[a, dest], sib_r.at[a, dest], sib
        ).wait_recv()

    def wait_line(a, dr, dest):
        ref = lrecv[a].at[dr, dest]
        remote(ref, ref, line_s.at[a, dr, dest], line_r.at[a, dr, dest], sib).wait_recv()

    def line_copy(a, dr, dest):
        return remote(
            srecv[a].at[dest],
            lrecv[a].at[dr, dest],
            line_s.at[a, dr, dest],
            line_r.at[a, dr, dest],
            (q, e + 2 if dr == 0 else e - 2),
        )

    def add_into(out, terms):
        rows = out.shape[0]
        step = min(rows, 16)

        @pl.loop(0, rows // step)
        def _(i):
            at = pl.ds(pl.multiple_of(i * step, step), step)
            total = terms[0][at, :].astype(jnp.float32)
            for t in terms[1:]:
                total = total + t[at, :].astype(jnp.float32)
            out[at, :] = total.astype(out.dtype)

    for i in range(CHIPS - 1):
        for a in range(3):
            for dr in range(2):
                if i == 0 and dr == 0:
                    if a == 0:
                        start_sib(1, 0)
                        start_sib(2, 0)
                        for w in range(3):
                            w_send(w, 1, shard_of(wp[w], dn, 0, half), xn)
                            w_send(w, 3, shard_of(wp[w], dn, half, half), yn)
                            w_send(w, 0, shard_of(wp[w], xn, 0, half), xn)
                            w_send(w, 2, shard_of(wp[w], yn, half, half), yn)
                    elif a == 1:
                        start_sib(0, 1)
                    else:
                        start_sib(1, 1)
                        start_sib(2, 1)
                dest = CHIPS - 1 - i if dr == 0 else i
                inner = z > 0 if dr == 0 else z < CHIPS - 1

                @pl.when(dest > z if dr == 0 else dest < z)
                def _():
                    wait_sib(a, dest)
                    mine, held = parts[a].at[2 * dest + c], srecv[a].at[dest]

                    @pl.when(inner)
                    def _():
                        wait_line(a, dr, dest)
                        add_into(held, (mine, held, lrecv[a].at[dr, dest]))

                    @pl.when(jnp.logical_not(inner))
                    def _():
                        add_into(held, (mine, held))

                    if i > 0:
                        line_copy(a, dr, dest + 1 if dr == 0 else dest - 1).wait_send()
                    line_copy(a, dr, dest).start()

        if i == 0:
            for w in range(3):
                held = wrecv[w].at[6]
                add_into(held, (shard_of(wp[w], yn, 0, half), w_got(w, 1)))
                w_send(w, 4, held, yn)
                held = wrecv[w].at[7]
                add_into(held, (shard_of(wp[w], xn, half, half), w_got(w, 3)))
                w_send(w, 5, held, xn)

    for w in range(3):
        for k in range(2):
            terms = (shard_of(wp[w], q, half * k, half), w_got(w, 2 * k), w_got(w, 4 + k))
            add_into(wout[w].at[pl.ds(half * k, half)], terms)

    for a in range(3):
        wait_sib(a, z)
        mine, other = parts[a].at[2 * z + c], srecv[a].at[z]

        @pl.when(z == 0)
        def _():
            wait_line(a, 1, z)
            add_into(outs[a], (mine, other, lrecv[a].at[1, z]))

        @pl.when(z == CHIPS - 1)
        def _():
            wait_line(a, 0, z)
            add_into(outs[a], (mine, other, lrecv[a].at[0, z]))

        @pl.when(jnp.logical_and(z > 0, z < CHIPS - 1))
        def _():
            wait_line(a, 0, z)
            wait_line(a, 1, z)
            add_into(outs[a], (mine, other, lrecv[a].at[0, z], lrecv[a].at[1, z]))

    for cp in w_copies:
        cp.wait_send()
    for i in range(CHIPS):
        for a in range(3):
            sib_copy(a, i).wait_send()
    for a in range(3):
        for i in range(CHIPS - 1):
            for dr in range(2):
                dest = CHIPS - 1 - i if dr == 0 else i
                pl.when(dest == z + 1 if dr == 0 else dest == z - 1)(
                    lambda: line_copy(a, dr, dest).wait_send()
                )


def reduce_all(parts, weight_parts):
    n, rows, width = parts[0].shape
    dma = pltpu.SemaphoreType.DMA
    vmem = pl.BlockSpec(memory_space=pltpu.VMEM)
    depth, hid = weight_parts[0].shape[1:]
    shards = [(depth, hid), (depth, hid), (hid, depth)]
    return pl.pallas_call(
        reduce_kernel,
        out_shape=tuple(jax.ShapeDtypeStruct(p.shape[1:], p.dtype) for p in parts)
        + tuple(jax.ShapeDtypeStruct(s, jnp.float32) for s in shards),
        in_specs=[vmem] * 6,
        out_specs=(vmem,) * 6,
        scratch_shapes=[pltpu.VMEM((CHIPS,) + p.shape[1:], p.dtype) for p in parts]
        + [pltpu.VMEM((2, CHIPS) + p.shape[1:], p.dtype) for p in parts]
        + [pltpu.VMEM((8, s[0] // 2, s[1]), jnp.bfloat16) for s in shards]
        + [dma((3, 4)), dma((3, 4)), dma((3, 2, 4)), dma((3, 2, 4)), dma((3, 6)), dma((3, 6))],
        compiler_params=pltpu.CompilerParams(
            collective_id=1, has_side_effects=True, vmem_limit_bytes=56 << 20
        ),
    )(*parts, *weight_parts)


def on_device(tokens, cotangent, expert_ids, gate_probs, w_gate, w_up, w_down):
    n = lax.axis_size("expert")
    rows, width = tokens.shape
    f32, bf16 = jnp.float32, jnp.bfloat16
    me = lax.axis_index("expert")
    named = expert_ids[None, :, :] == jnp.arange(n, dtype=jnp.int32)[:, None, None]
    weights_t = jnp.sum(jnp.where(named, gate_probs.astype(f32)[None], 0.0), axis=2)
    toks, cots, gates, full_gate, full_up, full_down = gather_all(
        tokens, cotangent, weights_t, w_gate[0], w_up[0], w_down[0]
    )
    x = toks.reshape(n * rows, width)
    cot = cots.reshape(n * rows, width)
    wg = full_gate.reshape(width, -1)
    wu = full_up.reshape(width, -1)
    g = lax.dynamic_index_in_dim(gates, me, axis=1, keepdims=False).reshape(n * rows, 1)
    dot = functools.partial(lax.dot_general, preferred_element_type=f32)
    mm, nt, tn = (((1,), (0,)), ((), ())), (((1,), (1,)), ((), ())), (((0,), (0,)), ((), ()))
    pre_gate = dot(x, wg, mm)
    pre_up = dot(x, wu, mm)
    back = dot(cot, full_down, nt)
    activated, slope = silu_parts(pre_gate)
    hidden = activated * pre_up
    weighted = (g * hidden).astype(bf16)
    gate_grad = jnp.sum(hidden * back, axis=1)
    grad_hidden = g * back
    grad_pre_gate = (grad_hidden * pre_up * slope).astype(bf16)
    grad_pre_up = (grad_hidden * activated).astype(bf16)
    part_mixed = dot(weighted, full_down, mm).astype(bf16).reshape(n, rows, width)
    part_tokens = (dot(grad_pre_gate, wg, nt) + dot(grad_pre_up, wu, nt)).astype(bf16)
    part_tokens = part_tokens.reshape(n, rows, width)
    part_gates = jnp.where(
        (jnp.arange(n) == me)[None, :, None], gate_grad.reshape(n, 1, rows), 0.0
    )
    part_gate_w = dot(x, grad_pre_gate, tn).astype(bf16).reshape(full_gate.shape)
    part_up_w = dot(x, grad_pre_up, tn).astype(bf16).reshape(full_up.shape)
    part_down_w = dot(weighted, cot, tn).astype(bf16)
    mixed, grad_tokens, gates_all, gw, uw, dw = reduce_all(
        (part_mixed, part_tokens, part_gates), (part_gate_w, part_up_w, part_down_w)
    )
    grad_gates = jnp.sum(jnp.where(named, gates_all[:, :, None], 0.0), axis=0)
    return (mixed, grad_tokens, grad_gates, gw[None], uw[None], dw[None])


def solution(mesh):
    small = mesh.shape["expert"] == 2 * CHIPS and mesh.shape["dp"] == 4
    in_specs = (
        P(("dp", "expert"), None),
        P(("dp", "expert"), None),
        P(("dp", "expert"), None),
        P(("dp", "expert"), None),
        P("expert", "dp", None),
        P("expert", "dp", None),
        P("expert", None, "dp"),
    )
    out_specs = (
        P(("dp", "expert"), None),
        P(("dp", "expert"), None),
        P(("dp", "expert"), None),
        P("expert", "dp", None),
        P("expert", "dp", None),
        P("expert", None, "dp"),
    )
    return jax.shard_map(
        on_device if small else on_device_routed,
        mesh=mesh,
        in_specs=in_specs,
        out_specs=out_specs,
        check_vma=False,
    )
```
